256 devices in a mesh: group: 8 (over z), dp: 2 (over x_hi), tp: 16 (over x_lo, y, core).
Axes of the slice: x: 4 (x_hi: 2, x_lo: 2; x = x_hi * 2 + x_lo), y: 4, z: 8, core: 2. Of those that a mesh axis runs over, the one named last changes fastest.
Arguments:
- token_step_inputs: bfloat16 [8, 2048, 16384], P(None, ('group', 'dp'), 'tp'), may hold values from -6 to 6
- key_value_weight: bfloat16 [16384, 2048], P('tp'), may hold values from -0.046875 to 0.046875
- adapter_down_factors: bfloat16 [64, 64, 16384], P(('group', 'dp'), None, 'tp'), may hold values from -0.046875 to 0.046875
- adapter_up_factors: bfloat16 [64, 64, 2048], P(('group', 'dp'), None, 'tp'), may hold values from -0.75 to 0.75
- block_owner_tenant: int32 [16], replicated, may hold values from 0 to 63
- queries: bfloat16 [8, 2048, 16384], P(None, ('group', 'dp', 'tp')), may hold values from -30 to 30
- key_value_cache: bfloat16 [2048, 32, 2048], P(('group', 'dp', 'tp')), may hold values from -6 to 6
- cache_length: int32 [2048], P(('group', 'dp', 'tp')), may hold values from 2 to 32, as said below
Outputs:
- attended: bfloat16 [8, 2048, 16384], P(None, ('group', 'dp', 'tp'))
The draws below stay inside these ranges and needn't reach their ends.
Inputs may be any that keep to these rules, and one draw needn't show every extreme that they name: `cache_length`: row r has length 32 whenever r is a multiple of 4.
All inputs are finite; a program needn't handle non-finite values.
Results may differ from the reference program's by a relative error of at most 0.0058.
Values may be sent and summed in bfloat16 or wider, within the bound.
No kernel may reach another device: no remote copies, remote signals or barrier semaphores. Data moves between devices by JAX's collectives and lax.ppermute only.
A program may use at most 128 MiB of HBM per device.

```python
import math
import jax
import jax.numpy as jnp
from jax import lax

MODEL_WIDTH = 16384
HQ = 128
KVH = 8
HD = 128
ADAPTER_RANK = 64
TENANT_COUNT = 64
BLOCK = 128
STEPS = 8
CACHE = 32
KEY_VALUE_WIDTH = 2048
NBLOCKS = 16
ROWS = 2048


def draw_queries(key, part):
    own_key = jax.random.fold_in(key, 5)
    values = jnp.clip(jax.random.normal(own_key, (STEPS, ROWS, HQ, HD), jnp.float32), -6.0, 6.0)
    return values.reshape(STEPS, ROWS, HQ * HD).astype(jnp.bfloat16)


def draw_key_value_cache(key, part):
    own_key = jax.random.fold_in(key, 6)
    cache_draw = jnp.clip(jax.random.normal(own_key, (ROWS, CACHE, 2, KVH, HD), jnp.float32), -6.0, 6.0)
    return cache_draw.reshape(ROWS, CACHE, 2 * KVH * HD).astype(jnp.bfloat16)


def draw_cache_length(key, part):
    own_key = jax.random.fold_in(key, 7)
    lengths = jax.random.randint(own_key, (ROWS,), 2, CACHE + 1, jnp.int32)
    row_index = jnp.arange(ROWS, dtype=jnp.int32)
    return jnp.where(row_index % 4 == 0, jnp.int32(CACHE), lengths).astype(jnp.int32)


def place_ends(entries, key, smallest, high):
    dims = entries.shape
    place = [jax.random.randint(jax.random.fold_in(key, axis), (), 0, dims[axis]) for axis in range(len(dims))]
    entries = entries.at[tuple(place)].set(smallest)
    longest = dims.index(max(dims))
    place[longest] = (place[longest] + 1) % dims[longest]
    return entries.at[tuple(place)].set(high)


def steps_of(rng, extent, shards, least, top_value):
    def one(position, blocks):
        draws = jax.random.uniform(jax.random.fold_in(jax.random.fold_in(rng, 6), position), (blocks,), jnp.float32, least / len(shards), top_value / len(shards))
        return jnp.repeat(jnp.exp(draws), extent[position] // blocks).reshape((-1,) + (1,) * (len(extent) - position - 1))

    gain = one(*shards[0])
    for cut in shards[1:]:
        gain = gain * one(*cut)
    return gain


def normal_values(stream_key, dims, width, reach, cuts=(), held_as=jnp.bfloat16):
    level = steps_of(stream_key, dims, cuts, -0.22, 0.18) if cuts else 1.0
    array = jax.random.normal(stream_key, dims, jnp.float32) * width * level
    return jnp.minimum(jnp.maximum(array, -reach), reach).astype(held_as)


def setup_inputs(seed: int = 0) -> dict:
    arg_keys = jax.random.split(jax.random.key(seed), 9)
    token_step_inputs = normal_values(arg_keys[0], (STEPS, ROWS, MODEL_WIDTH), 1.0, 6.0, ((1, 16), (2, 16)))
    key_value_weight = normal_values(arg_keys[1], (MODEL_WIDTH, KEY_VALUE_WIDTH), MODEL_WIDTH ** -0.5, 0.046875, ((0, 16),))
    adapter_down_factors = normal_values(arg_keys[2], (TENANT_COUNT, ADAPTER_RANK, MODEL_WIDTH), MODEL_WIDTH ** -0.5, 0.046875, ((0, 16), (2, 16)))
    adapter_up_factors = normal_values(arg_keys[3], (TENANT_COUNT, ADAPTER_RANK, KEY_VALUE_WIDTH), ADAPTER_RANK ** -0.5, 0.75, ((0, 16), (2, 16)))
    block_owner_tenant = place_ends(jax.random.randint(arg_keys[4], (NBLOCKS,), 0, TENANT_COUNT), jax.random.fold_in(arg_keys[4], 1), 0, TENANT_COUNT - 1).astype(jnp.int32)
    queries = draw_queries(jax.random.fold_in(arg_keys[8], 71), 0)
    key_value_cache = draw_key_value_cache(jax.random.fold_in(arg_keys[8], 71), 0)
    cache_length = draw_cache_length(jax.random.fold_in(arg_keys[8], 71), 0)
    return dict(token_step_inputs=token_step_inputs, key_value_weight=key_value_weight, adapter_down_factors=adapter_down_factors, adapter_up_factors=adapter_up_factors, block_owner_tenant=block_owner_tenant, queries=queries, key_value_cache=key_value_cache, cache_length=cache_length)


masked_value = -1e+30

def attend(query_rows, cache_rows, lengths, new_key_value):
    step_count = query_rows.shape[0]
    row_count = query_rows.shape[1]
    group_size = HQ // KVH
    half_width = KVH * HD
    score_scale = 1.0 / math.sqrt(HD)
    upper_bound = lax.Precision.HIGHEST
    query_heads = query_rows.astype(jnp.float32).reshape(step_count, row_count, KVH, group_size, HD)
    cache_keys = cache_rows[:, :, :half_width].astype(jnp.float32).reshape(row_count, CACHE, KVH, HD)
    cache_vals = cache_rows[:, :, half_width:].astype(jnp.float32).reshape(row_count, CACHE, KVH, HD)
    fresh_keys = new_key_value[:, :, :half_width].astype(jnp.float32).reshape(step_count, row_count, KVH, HD)
    fresh_vals = new_key_value[:, :, half_width:].astype(jnp.float32).reshape(step_count, row_count, KVH, HD)
    cache_scores = jnp.einsum('smhgd,mchd->smhgc', query_heads, cache_keys, precision=upper_bound) * score_scale
    fresh_scores = jnp.einsum('smhgd,tmhd->smhgt', query_heads, fresh_keys, precision=upper_bound) * score_scale
    cache_mask = jnp.arange(CACHE, dtype=jnp.int32)[None, :] < lengths[:, None]
    cache_scores = jnp.where(cache_mask[None, :, None, None, :], cache_scores, masked_value)
    fresh_mask = jnp.arange(step_count, dtype=jnp.int32)[None, :] <= jnp.arange(step_count, dtype=jnp.int32)[:, None]
    fresh_scores = jnp.where(fresh_mask[:, None, None, None, :], fresh_scores, masked_value)
    row_max = jnp.maximum(cache_scores.max(-1), fresh_scores.max(-1))[..., None]
    cache_exp = jnp.exp(cache_scores - row_max)
    fresh_exp = jnp.exp(fresh_scores - row_max)
    exp_total = cache_exp.sum(-1, keepdims=True) + fresh_exp.sum(-1, keepdims=True)
    cache_probs = (cache_exp / exp_total).astype(jnp.bfloat16).astype(jnp.float32)
    fresh_probs = (fresh_exp / exp_total).astype(jnp.bfloat16).astype(jnp.float32)
    mixed_out = jnp.einsum('smhgc,mchd->smhgd', cache_probs, cache_vals, precision=upper_bound)
    mixed_out = mixed_out + jnp.einsum('smhgt,tmhd->smhgd', fresh_probs, fresh_vals, precision=upper_bound)
    return mixed_out.reshape(step_count, row_count, HQ * HD).astype(jnp.bfloat16)

def reference(token_step_inputs, key_value_weight, adapter_down_factors, adapter_up_factors, block_owner_tenant, queries, key_value_cache, cache_length):
    upper_bound = lax.Precision.HIGHEST
    block_count = block_owner_tenant.shape[0]
    weight_wide = key_value_weight.astype(jnp.float32)

    def one_block(block_index):
        row_start = (block_index * BLOCK).astype(jnp.int32)
        input_rows = lax.dynamic_slice_in_dim(token_step_inputs, row_start, BLOCK, 1).astype(jnp.float32)
        tenant_index = block_owner_tenant[block_index].astype(jnp.int32)
        block_down_factor = lax.dynamic_index_in_dim(adapter_down_factors, tenant_index, 0, keepdims=False).astype(jnp.float32)
        block_up_factor = lax.dynamic_index_in_dim(adapter_up_factors, tenant_index, 0, keepdims=False).astype(jnp.float32)
        rank_projection = jnp.einsum('cfh,qh->cfq', input_rows, block_down_factor, precision=upper_bound)
        base_output = jnp.einsum('sbd,dk->sbk', input_rows, weight_wide, precision=upper_bound)
        new_key_value = (base_output + jnp.einsum('jwv,vt->jwt', rank_projection, block_up_factor, precision=upper_bound)).astype(jnp.bfloat16)
        query_rows = lax.dynamic_slice_in_dim(queries, row_start, BLOCK, 1)
        cache_rows = lax.dynamic_slice_in_dim(key_value_cache, row_start, BLOCK, 0)
        lengths = lax.dynamic_slice_in_dim(cache_length, row_start, BLOCK, 0)
        return attend(query_rows, cache_rows, lengths, new_key_value)
    per_block = lax.map(one_block, jnp.arange(block_count, dtype=jnp.int32))
    return jnp.transpose(per_block, (1, 0, 2, 3)).reshape(STEPS, block_count * BLOCK, HQ * HD)
```

```python
import functools
import math

import jax
import jax.numpy as jnp
from jax import lax
from jax.experimental import pallas as pl
from jax.experimental.pallas import tpu as pltpu
from jax.sharding import PartitionSpec as P

KVH = 8
HD = 128
GROUP = 16
STEPS = 8
OWN_ROWS = 8
TOKENS = STEPS * OWN_ROWS
CACHED = 32
MODEL_SHARD = 1024
RANK = 64
HALF_WIDTH = KVH * HD
PART_WIDTHS = (512, 768, 768)
PART_ORDERS = (("x", "u", "v"), ("u", "v", "x"), ("v", "x", "u"))
MASKED = -1e30
SCORE_SCALE = math.log2(math.e) / math.sqrt(HD)
MIB = 1 << 20


def tp_position(x, y, core):
    return (x * 4 + y) * 2 + core


def tp_pairs(move):
    return [
        (tp_position(x, y, core), tp_position(*move(x, y, core)))
        for x in range(2)
        for y in range(4)
        for core in range(2)
    ]


PAIRS = {
    "core": tp_pairs(lambda x, y, core: (x, y, 1 - core)),
    "x": tp_pairs(lambda x, y, core: (1 - x, y, core)),
    "u": tp_pairs(lambda x, y, core: (x, y ^ 1, core)),
    "v": tp_pairs(lambda x, y, core: (x, 3 - y, core)),
}
RING = (0, 1, 3, 2)


def swap(array, dim):
    return lax.ppermute(array, "tp", PAIRS[dim])


def half(array, axis, index):
    return lax.dynamic_index_in_dim(array, index, axis, keepdims=True)


def project_kernel(core_ref, inputs_ref, weight_ref, keep_ref, send_ref):
    first = core_ref[0] == 0
    product = jnp.dot(
        inputs_ref[...].reshape(STEPS * 128, MODEL_SHARD),
        weight_ref[...],
        preferred_element_type=jnp.float32,
    )
    width = product.shape[1]
    product = product.reshape(STEPS, 8, 2, OWN_ROWS, width)
    for x in range(2):
        for v in range(2):
            for u in range(2):
                chip = x * 4 + RING[v * 2 + u]
                even = product[:, chip, 0].reshape(TOKENS, width)
                odd = product[:, chip, 1].reshape(TOKENS, width)
                keep_ref[x, v, u] = jnp.where(first, even, odd)
                send_ref[x, v, u] = jnp.where(first, odd, even).astype(jnp.bfloat16)


def project(core, token_step_inputs, key_value_weight, start, width):
    block = 256
    first_block = start // block
    out_shape = (2, 2, 2, TOKENS, width)
    out_spec = pl.BlockSpec((2, 2, 2, TOKENS, block), lambda n, core_ref: (0, 0, 0, 0, n))
    return pl.pallas_call(
        project_kernel,
        grid_spec=pltpu.PrefetchScalarGridSpec(
            num_scalar_prefetch=1,
            grid=(width // block,),
            in_specs=[
                pl.BlockSpec((STEPS, 128, MODEL_SHARD), lambda n, core_ref: (0, 0, 0)),
                pl.BlockSpec((MODEL_SHARD, block), lambda n, core_ref: (0, n + first_block)),
            ],
            out_specs=[out_spec, out_spec],
        ),
        out_shape=[
            jax.ShapeDtypeStruct(out_shape, jnp.float32),
            jax.ShapeDtypeStruct(out_shape, jnp.bfloat16),
        ],
        compiler_params=pltpu.CompilerParams(vmem_limit_bytes=40 * MIB),
        cost_estimate=pl.CostEstimate(
            flops=2 * 1024 * MODEL_SHARD * width,
            bytes_accessed=2 * MIB + 2 * MODEL_SHARD * width + 6 * 512 * width,
            transcendentals=0,
        ),
        name="project",
    )(core, token_step_inputs, key_value_weight)


def reduce_part(keep, received, order, bits):
    axis_of = {"x": 0, "v": 1, "u": 2}
    for dim in order:
        axis, bit = axis_of[dim], bits[dim]
        outgoing = (
            half(keep, axis, 1 - bit) + half(received, axis, 1 - bit).astype(jnp.float32)
        ).astype(jnp.bfloat16)
        arriving = swap(outgoing, dim)
        keep = half(keep, axis, bit) + half(received, axis, bit).astype(jnp.float32)
        received = arriving
    return keep.reshape(TOKENS, -1), received.reshape(TOKENS, -1)


def route_factors(factors, owners, group, dp):
    shard = group * 2 + dp
    rank_half = RANK // 2
    up_ring = [(i, (i + 1) % 8) for i in range(8)]
    down_ring = [(i, (i - 1) % 8) for i in range(8)]

    def slot(offset, part):
        target = lax.rem(group + offset + 8, 8)
        slots = []
        for target_dp in range(2):
            tenant = owners[target * 2 + target_dp]
            mine = (tenant // 4) == shard
            held = lax.dynamic_slice(
                factors,
                (lax.rem(tenant, 4), part * rank_half, 0),
                (1, rank_half, factors.shape[2]),
            )
            slots.append((mine, held))
        return slots

    def fill(slots, arrived):
        rows = []
        for i, (mine, held) in enumerate(slots):
            other = jnp.zeros_like(held) if arrived is None else arrived[i : i + 1]
            rows.append(jnp.where(mine, held, other))
        return jnp.concatenate(rows, axis=0)

    chains = []
    for part in range(2):
        for sign, ring in ((1, up_ring), (-1, down_ring)):
            hops = 4 if (part == 0) == (sign == 1) else 3
            chains.append([part, sign, ring, hops, None])
    for hop in range(4, 0, -1):
        for chain in chains:
            part, sign, ring, hops, arrived = chain
            if hop <= hops:
                outgoing = fill(slot(sign * hop, part), arrived)
                chain[4] = lax.ppermute(outgoing, "group", ring)
    parts = []
    for part in range(2):
        arrivals = [chain[4] for chain in chains if chain[0] == part]
        parts.append(fill(slot(0, part), arrivals[0] + arrivals[1]))
    collected = jnp.concatenate(parts, axis=1)
    outgoing = lax.dynamic_index_in_dim(collected, 1 - dp, 0, keepdims=False)
    kept = lax.dynamic_index_in_dim(collected, dp, 0, keepdims=False)
    arrived = lax.ppermute(outgoing, "dp", [(0, 1), (1, 0)])
    tenant = owners[shard]
    here = lax.rem(tenant // 4, 2) == dp
    return jnp.where(here, kept, arrived)


def gather_up(up_slice):
    held = up_slice[None]
    for dim in ("core", "u", "v", "x"):
        held = jnp.concatenate([held, swap(held, dim)], axis=0)
    return held


def low_kernel(inputs_ref, down_ref, low_ref):
    product = lax.dot_general(
        inputs_ref[...].reshape(STEPS * 128, MODEL_SHARD),
        down_ref[...],
        (((1,), (1,)), ((), ())),
        preferred_element_type=jnp.float32,
    )
    product = product.reshape(STEPS, 16, OWN_ROWS, RANK)
    for device in range(16):
        low_ref[device] = product[:, device].reshape(TOKENS, RANK)


def low_rank(token_step_inputs, down):
    return pl.pallas_call(
        low_kernel,
        out_shape=jax.ShapeDtypeStruct((16, TOKENS, RANK), jnp.float32),
        compiler_params=pltpu.CompilerParams(vmem_limit_bytes=24 * MIB),
        cost_estimate=pl.CostEstimate(
            flops=2 * 1024 * MODEL_SHARD * RANK, bytes_accessed=3 * MIB, transcendentals=0
        ),
        name="low_rank",
    )(token_step_inputs, down)


def scatter_low(low_parts, tp):
    total = lax.dynamic_index_in_dim(low_parts, tp, 0, keepdims=False)
    for offset in range(1, 16):
        outgoing = lax.dynamic_index_in_dim(low_parts, tp ^ offset, 0, keepdims=False)
        total = total + lax.ppermute(outgoing, "tp", [(i, i ^ offset) for i in range(16)])
    return total


def attend_kernel(
    slots_ref, lengths_ref, queries_ref, cache_keys_ref, cache_values_ref, low_ref, up_ref, *rest
):
    base_refs, (out_ref, fresh_ref) = rest[:6], rest[6:]
    head = pl.program_id(0)

    @pl.when(head == 0)
    def _():
        low = low_ref[...]
        coarse = low.astype(jnp.bfloat16)
        fine = (low - coarse.astype(jnp.float32)).astype(jnp.bfloat16)
        column = 0
        for part, width in enumerate(PART_WIDTHS):
            keep_ref, received_ref = base_refs[2 * part], base_refs[2 * part + 1]
            for start in range(0, width, HD):
                up = up_ref[slots_ref[column // HD]]
                adapter = jnp.dot(coarse, up, preferred_element_type=jnp.float32)
                adapter = adapter + jnp.dot(fine, up, preferred_element_type=jnp.float32)
                base = keep_ref[:, start : start + HD] + received_ref[
                    :, start : start + HD
                ].astype(jnp.float32)
                fresh_ref[column // HD] = (base + adapter).astype(jnp.bfloat16)
                column += HD

    rows = GROUP * TOKENS
    queries = queries_ref[...].astype(jnp.float32).reshape(TOKENS, GROUP * HD).astype(jnp.bfloat16)
    queries = jnp.concatenate([queries[:, g * HD : (g + 1) * HD] for g in range(GROUP)], axis=0)

    def scores_of(keys):
        return lax.dot_general(
            queries, keys, (((1,), (1,)), ((), ())), preferred_element_type=jnp.float32
        )

    def with_ones(values):
        return jnp.concatenate([values, jnp.ones_like(values)], axis=1)

    row = lax.broadcasted_iota(jnp.int32, (OWN_ROWS, OWN_ROWS * CACHED), 0)
    column = lax.broadcasted_iota(jnp.int32, (OWN_ROWS, OWN_ROWS * CACHED), 1)
    limit = jnp.zeros_like(row)
    for m in range(OWN_ROWS):
        limit = jnp.where(row == m, lengths_ref[m], limit)
    admitted = (column // CACHED == row) & (column % CACHED < limit)
    cache_bias = jnp.where(admitted, 0.0, MASKED)
    row = lax.broadcasted_iota(jnp.int32, (TOKENS, TOKENS), 0)
    column = lax.broadcasted_iota(jnp.int32, (TOKENS, TOKENS), 1)
    admitted = (column % OWN_ROWS == row % OWN_ROWS) & (column // OWN_ROWS <= row // OWN_ROWS)
    fresh_bias = jnp.where(admitted, 0.0, MASKED)

    cache_scores = scores_of(cache_keys_ref[...].reshape(OWN_ROWS * CACHED, HD))
    cache_scores = (
        cache_scores.reshape(rows // OWN_ROWS, OWN_ROWS, -1) * SCORE_SCALE + cache_bias[None]
    ).reshape(rows, -1)
    fresh_scores = scores_of(fresh_ref[head])
    fresh_scores = (
        fresh_scores.reshape(GROUP, TOKENS, TOKENS) * SCORE_SCALE + fresh_bias[None]
    ).reshape(rows, -1)
    row_max = jnp.maximum(
        cache_scores.max(-1, keepdims=True), fresh_scores.max(-1, keepdims=True)
    )
    cache_probs = jnp.exp2(cache_scores - row_max).astype(jnp.bfloat16)
    fresh_probs = jnp.exp2(fresh_scores - row_max).astype(jnp.bfloat16)
    mixed = jnp.dot(
        cache_probs,
        with_ones(cache_values_ref[...].reshape(OWN_ROWS * CACHED, HD)),
        preferred_element_type=jnp.float32,
    )
    mixed = mixed + jnp.dot(
        fresh_probs, with_ones(fresh_ref[KVH + head]), preferred_element_type=jnp.float32
    )
    mixed = (mixed[:, :HD] / mixed[:, HD:]).reshape(GROUP, STEPS, OWN_ROWS, HD)
    for g in range(GROUP):
        out_ref[:, :, g * HD : (g + 1) * HD] = mixed[g].astype(jnp.bfloat16)


def attend(slots, lengths, queries, cache, low, up, bases):
    def whole(array):
        return pl.BlockSpec(array.shape, lambda h, *_: (0,) * array.ndim)

    heads_spec = pl.BlockSpec((STEPS, OWN_ROWS, GROUP * HD), lambda h, *_: (0, 0, h))
    return pl.pallas_call(
        attend_kernel,
        grid_spec=pltpu.PrefetchScalarGridSpec(
            num_scalar_prefetch=2,
            grid=(KVH,),
            in_specs=[
                heads_spec,
                pl.BlockSpec((OWN_ROWS, CACHED, HD), lambda h, *_: (0, 0, h)),
                pl.BlockSpec((OWN_ROWS, CACHED, HD), lambda h, *_: (0, 0, KVH + h)),
                whole(low),
                whole(up),
                *[whole(base) for base in bases],
            ],
            out_specs=heads_spec,
            scratch_shapes=[pltpu.VMEM((2 * KVH, TOKENS, HD), jnp.bfloat16)],
        ),
        out_shape=jax.ShapeDtypeStruct(queries.shape, jnp.bfloat16),
        compiler_params=pltpu.CompilerParams(vmem_limit_bytes=40 * MIB),
        cost_estimate=pl.CostEstimate(
            flops=8 * MIB * 1024, bytes_accessed=8 * MIB, transcendentals=4 * MIB
        ),
        name="attend",
    )(slots, lengths, queries, cache, cache, low, up, *bases)


def shards(
    token_step_inputs,
    key_value_weight,
    adapter_down_factors,
    adapter_up_factors,
    block_owner_tenant,
    queries,
    key_value_cache,
    cache_length,
):
    group, dp, tp = (lax.axis_index(name) for name in ("group", "dp", "tp"))
    core, y, x = tp % 2, (tp // 2) % 4, tp // 8
    bits = {
        "x": x,
        "u": ((y == 1) | (y == 2)).astype(jnp.int32),
        "v": (y >= 2).astype(jnp.int32),
    }

    factors = jnp.concatenate([adapter_down_factors, adapter_up_factors], axis=2)
    mine = route_factors(factors, block_owner_tenant, group, dp)
    down, up_slice = mine[:, :MODEL_SHARD], mine[:, MODEL_SHARD:]

    core_id = core.astype(jnp.int32).reshape(1)
    bases = []
    start = 0
    for width, order in zip(PART_WIDTHS, PART_ORDERS):
        keep, outgoing = project(core_id, token_step_inputs, key_value_weight, start, width)
        received = swap(outgoing, "core")
        bases.extend(reduce_part(keep, received, order, bits))
        start += width

    up = gather_up(up_slice)
    low = scatter_low(low_rank(token_step_inputs, down), tp)

    column_owner = jnp.arange(16, dtype=jnp.int32)
    owner_y = (column_owner // 2) % 4
    slots = (
        ((column_owner % 2) ^ core)
        + 2 * (((owner_y == 1) | (owner_y == 2)).astype(jnp.int32) ^ bits["u"])
        + 4 * ((owner_y >= 2).astype(jnp.int32) ^ bits["v"])
        + 8 * ((column_owner // 8) ^ x)
    ).astype(jnp.int32)
    return attend(slots, cache_length, queries, key_value_cache, low, up, bases)


def solution(mesh):
    in_specs = (
        P(None, ("group", "dp"), "tp"),
        P("tp", None),
        P(("group", "dp"), None, "tp"),
        P(("group", "dp"), None, "tp"),
        P(),
        P(None, ("group", "dp", "tp"), None),
        P(("group", "dp", "tp"), None, None),
        P(("group", "dp", "tp")),
    )
    out_specs = P(None, ("group", "dp", "tp"), None)
    return jax.shard_map(shards, mesh=mesh, in_specs=in_specs, out_specs=out_specs, check_vma=False)
```

```python
import math

import jax
import jax.numpy as jnp
from jax import lax
from jax.experimental import pallas as pl
from jax.experimental.pallas import tpu as pltpu
from jax.sharding import PartitionSpec as P

KVH = 8
HD = 128
GROUP = 16
STEPS = 8
OWN_ROWS = 8
TOKENS = STEPS * OWN_ROWS
CACHED = 32
MODEL_SHARD = 1024
RANK = 64
HALF_WIDTH = KVH * HD
PART_WIDTHS = (1024, 1024)
PART_ORDERS = (("x", "u", "v"), ("u", "v", "x"))
MASKED = -1e30
SCORE_SCALE = math.log2(math.e) / math.sqrt(HD)
MIB = 1 << 20


def tp_position(x, y, core):
    return (x * 4 + y) * 2 + core


def tp_pairs(move):
    return [
        (tp_position(x, y, core), tp_position(*move(x, y, core)))
        for x in range(2)
        for y in range(4)
        for core in range(2)
    ]


PAIRS = {
    "core": tp_pairs(lambda x, y, core: (x, y, 1 - core)),
    "x": tp_pairs(lambda x, y, core: (1 - x, y, core)),
    "u": tp_pairs(lambda x, y, core: (x, y ^ 1, core)),
    "v": tp_pairs(lambda x, y, core: (x, 3 - y, core)),
}
RING = (0, 1, 3, 2)


def swap(array, dim):
    return lax.ppermute(array, "tp", PAIRS[dim])


def half(array, axis, index):
    return lax.dynamic_index_in_dim(array, index, axis, keepdims=True)


def project_kernel(core_ref, inputs_ref, weight_ref, keep_ref, send_ref):
    first = core_ref[0] == 0
    product = jnp.dot(
        inputs_ref[...].reshape(STEPS * 128, MODEL_SHARD),
        weight_ref[...],
        preferred_element_type=jnp.float32,
    )
    width = product.shape[1]
    product = product.reshape(STEPS, 8, 2, OWN_ROWS, width)
    for x in range(2):
        for v in range(2):
            for u in range(2):
                chip = x * 4 + RING[v * 2 + u]
                even = product[:, chip, 0].reshape(TOKENS, width)
                odd = product[:, chip, 1].reshape(TOKENS, width)
                keep_ref[x, v, u] = jnp.where(first, even, odd)
                send_ref[x, v, u] = jnp.where(first, odd, even).astype(jnp.bfloat16)


def project(core, token_step_inputs, key_value_weight, start, width):
    block = 256
    first_block = start // block
    out_shape = (2, 2, 2, TOKENS, width)
    out_spec = pl.BlockSpec((2, 2, 2, TOKENS, block), lambda n, core_ref: (0, 0, 0, 0, n))
    return pl.pallas_call(
        project_kernel,
        grid_spec=pltpu.PrefetchScalarGridSpec(
            num_scalar_prefetch=1,
            grid=(width // block,),
            in_specs=[
                pl.BlockSpec((STEPS, 128, MODEL_SHARD), lambda n, core_ref: (0, 0, 0)),
                pl.BlockSpec((MODEL_SHARD, block), lambda n, core_ref: (0, n + first_block)),
            ],
            out_specs=[out_spec, out_spec],
        ),
        out_shape=[
            jax.ShapeDtypeStruct(out_shape, jnp.float32),
            jax.ShapeDtypeStruct(out_shape, jnp.bfloat16),
        ],
        compiler_params=pltpu.CompilerParams(vmem_limit_bytes=40 * MIB),
        cost_estimate=pl.CostEstimate(
            flops=2 * 1024 * MODEL_SHARD * width,
            bytes_accessed=2 * MIB + 2 * MODEL_SHARD * width + 6 * 512 * width,
            transcendentals=0,
        ),
        name="project",
    )(core, token_step_inputs, key_value_weight)


def reduce_part(keep, received, order, bits):
    axis_of = {"x": 0, "v": 1, "u": 2}
    for dim in order:
        axis, bit = axis_of[dim], bits[dim]
        outgoing = (
            half(keep, axis, 1 - bit) + half(received, axis, 1 - bit).astype(jnp.float32)
        ).astype(jnp.bfloat16)
        arriving = swap(outgoing, dim)
        keep = half(keep, axis, bit) + half(received, axis, bit).astype(jnp.float32)
        received = arriving
    return keep.reshape(TOKENS, -1), received.reshape(TOKENS, -1)


def slots_kernel(owners_ref, shard_ref, down_ref, up_ref, out_ref):
    for block in range(16):
        tenant = owners_ref[block]
        mine = tenant // 4 == shard_ref[0]
        held = lax.rem(tenant, 4)
        down, up = down_ref[held], up_ref[held]
        out_ref[block, :, :MODEL_SHARD] = jnp.where(mine, down, jnp.zeros_like(down))
        out_ref[block, :, MODEL_SHARD:] = jnp.where(mine, up, jnp.zeros_like(up))


def factor_slots(owners, shard, down, up):
    smem = pl.BlockSpec(memory_space=pltpu.SMEM)
    vmem = pl.BlockSpec(memory_space=pltpu.VMEM)
    return pl.pallas_call(
        slots_kernel,
        in_specs=[smem, smem, vmem, vmem],
        out_specs=vmem,
        out_shape=jax.ShapeDtypeStruct((16, RANK, MODEL_SHARD + HD), jnp.bfloat16),
        cost_estimate=pl.CostEstimate(flops=0, bytes_accessed=5 * MIB, transcendentals=0),
        name="factor_slots",
    )(owners, shard, down, up)


def low_kernel(here_ref, inputs_ref, kept_ref, arrived_ref, out_ref):
    factors = jnp.where(here_ref[0] == 1, kept_ref[...], arrived_ref[...])
    product = lax.dot_general(
        inputs_ref[...].reshape(STEPS * 128, MODEL_SHARD),
        factors[:, :MODEL_SHARD],
        (((1,), (1,)), ((), ())),
        preferred_element_type=jnp.float32,
    )
    product = product.reshape(STEPS, 16, OWN_ROWS, RANK)
    for device in range(16):
        rows = product[:, device].reshape(2, TOKENS // 2, RANK)
        rows = jnp.concatenate([rows[0], rows[1]], axis=1)
        out_ref[device, : TOKENS // 2] = rows.astype(jnp.bfloat16)
        out_ref[device, TOKENS // 2 :] = factors[:, MODEL_SHARD:]


def low_rank(here, token_step_inputs, kept, arrived):
    vmem = pl.BlockSpec(memory_space=pltpu.VMEM)
    return pl.pallas_call(
        low_kernel,
        in_specs=[pl.BlockSpec(memory_space=pltpu.SMEM), vmem, vmem, vmem],
        out_specs=vmem,
        out_shape=jax.ShapeDtypeStruct((16, TOKENS // 2 + RANK, HD), jnp.bfloat16),
        compiler_params=pltpu.CompilerParams(vmem_limit_bytes=24 * MIB),
        cost_estimate=pl.CostEstimate(
            flops=2 * 1024 * MODEL_SHARD * RANK, bytes_accessed=3 * MIB, transcendentals=0
        ),
        name="low_rank",
    )(here, token_step_inputs, kept, arrived)


def attend_kernel(
    lengths_ref, queries_ref, cache_keys_ref, cache_values_ref, adapter_ref, *rest
):
    base_refs, (out_ref, fresh_ref) = rest[:-2], rest[-2:]
    head = pl.program_id(0)

    @pl.when(head == 0)
    def _():
        low = adapter_ref[0, : TOKENS // 2].astype(jnp.float32)
        for device in range(1, 16):
            low = low + adapter_ref[device, : TOKENS // 2].astype(jnp.float32)
        low = jnp.concatenate([low[:, :RANK], low[:, RANK:]], axis=0)
        coarse = low.astype(jnp.bfloat16)
        fine = (low - coarse.astype(jnp.float32)).astype(jnp.bfloat16)
        column = 0
        for part, width in enumerate(PART_WIDTHS):
            keep_ref, received_ref = base_refs[2 * part], base_refs[2 * part + 1]
            for start in range(0, width, HD):
                up = adapter_ref[column // HD, TOKENS // 2 :]
                adapter = jnp.dot(coarse, up, preferred_element_type=jnp.float32)
                adapter = adapter + jnp.dot(fine, up, preferred_element_type=jnp.float32)
                base = keep_ref[:, start : start + HD] + received_ref[
                    :, start : start + HD
                ].astype(jnp.float32)
                fresh_ref[column // HD] = (base + adapter).astype(jnp.bfloat16)
                column += HD

    rows = GROUP * TOKENS
    queries = queries_ref[...].astype(jnp.float32).reshape(TOKENS, GROUP * HD).astype(jnp.bfloat16)
    queries = jnp.concatenate([queries[:, g * HD : (g + 1) * HD] for g in range(GROUP)], axis=0)

    def scores_of(keys):
        return lax.dot_general(
            queries, keys, (((1,), (1,)), ((), ())), preferred_element_type=jnp.float32
        )

    def with_ones(values):
        return jnp.concatenate([values, jnp.ones_like(values)], axis=1)

    row = lax.broadcasted_iota(jnp.int32, (OWN_ROWS, OWN_ROWS * CACHED), 0)
    column = lax.broadcasted_iota(jnp.int32, (OWN_ROWS, OWN_ROWS * CACHED), 1)
    limit = jnp.zeros_like(row)
    for m in range(OWN_ROWS):
        limit = jnp.where(row == m, lengths_ref[m], limit)
    admitted = (column // CACHED == row) & (column % CACHED < limit)
    cache_bias = jnp.where(admitted, 0.0, MASKED)
    row = lax.broadcasted_iota(jnp.int32, (TOKENS, TOKENS), 0)
    column = lax.broadcasted_iota(jnp.int32, (TOKENS, TOKENS), 1)
    admitted = (column % OWN_ROWS == row % OWN_ROWS) & (column // OWN_ROWS <= row // OWN_ROWS)
    fresh_bias = jnp.where(admitted, 0.0, MASKED)

    cache_scores = scores_of(cache_keys_ref[...].reshape(OWN_ROWS * CACHED, HD))
    cache_scores = (
        cache_scores.reshape(rows // OWN_ROWS, OWN_ROWS, -1) * SCORE_SCALE + cache_bias[None]
    ).reshape(rows, -1)
    fresh_scores = scores_of(fresh_ref[head])
    fresh_scores = (
        fresh_scores.reshape(GROUP, TOKENS, TOKENS) * SCORE_SCALE + fresh_bias[None]
    ).reshape(rows, -1)
    row_max = jnp.maximum(
        cache_scores.max(-1, keepdims=True), fresh_scores.max(-1, keepdims=True)
    )
    cache_probs = jnp.exp2(cache_scores - row_max).astype(jnp.bfloat16)
    fresh_probs = jnp.exp2(fresh_scores - row_max).astype(jnp.bfloat16)
    mixed = jnp.dot(
        cache_probs,
        with_ones(cache_values_ref[...].reshape(OWN_ROWS * CACHED, HD)),
        preferred_element_type=jnp.float32,
    )
    mixed = mixed + jnp.dot(
        fresh_probs, with_ones(fresh_ref[KVH + head]), preferred_element_type=jnp.float32
    )
    mixed = (mixed[:, :HD] / mixed[:, HD:]).reshape(GROUP, STEPS, OWN_ROWS, HD)
    for g in range(GROUP):
        out_ref[:, :, g * HD : (g + 1) * HD] = mixed[g].astype(jnp.bfloat16)


def attend(lengths, queries, cache, adapter, bases):
    def whole(array):
        return pl.BlockSpec(array.shape, lambda h, *_: (0,) * array.ndim)

    heads_spec = pl.BlockSpec((STEPS, OWN_ROWS, GROUP * HD), lambda h, *_: (0, 0, h))
    return pl.pallas_call(
        attend_kernel,
        grid_spec=pltpu.PrefetchScalarGridSpec(
            num_scalar_prefetch=1,
            grid=(KVH,),
            in_specs=[
                heads_spec,
                pl.BlockSpec((OWN_ROWS, CACHED, HD), lambda h, *_: (0, 0, h)),
                pl.BlockSpec((OWN_ROWS, CACHED, HD), lambda h, *_: (0, 0, KVH + h)),
                whole(adapter),
                *[whole(base) for base in bases],
            ],
            out_specs=heads_spec,
            scratch_shapes=[pltpu.VMEM((2 * KVH, TOKENS, HD), jnp.bfloat16)],
        ),
        out_shape=jax.ShapeDtypeStruct(queries.shape, jnp.bfloat16),
        compiler_params=pltpu.CompilerParams(vmem_limit_bytes=40 * MIB),
        cost_estimate=pl.CostEstimate(
            flops=8 * MIB * 1024, bytes_accessed=8 * MIB, transcendentals=4 * MIB
        ),
        name="attend",
    )(lengths, queries, cache, cache, adapter, *bases)


def shards(
    token_step_inputs,
    key_value_weight,
    adapter_down_factors,
    adapter_up_factors,
    block_owner_tenant,
    queries,
    key_value_cache,
    cache_length,
):
    group, dp, tp = (lax.axis_index(name) for name in ("group", "dp", "tp"))
    core, y, x = tp % 2, (tp // 2) % 4, tp // 8
    bits = {
        "x": x,
        "u": ((y == 1) | (y == 2)).astype(jnp.int32),
        "v": (y >= 2).astype(jnp.int32),
    }

    shard = group * 2 + dp
    slots = factor_slots(
        block_owner_tenant, shard.reshape(1), adapter_down_factors, adapter_up_factors
    )
    slots = slots.reshape(8, 2, RANK, slots.shape[2])
    slots = lax.psum_scatter(slots, "group", scatter_dimension=0, tiled=True)[0]

    core_id = core.reshape(1)
    bases = []
    start = 0
    for width, order in zip(PART_WIDTHS, PART_ORDERS):
        keep, outgoing = project(core_id, token_step_inputs, key_value_weight, start, width)
        bases.extend(reduce_part(keep, swap(outgoing, "core"), order, bits))
        start += width

    here = (lax.rem(block_owner_tenant[shard] // 4, 2) == dp).astype(jnp.int32).reshape(1)
    kept = lax.dynamic_index_in_dim(slots, dp, 0, keepdims=False)
    outgoing = lax.dynamic_index_in_dim(slots, 1 - dp, 0, keepdims=False)
    arrived = lax.ppermute(outgoing, "dp", [(0, 1), (1, 0)])
    adapter = lax.all_to_all(
        low_rank(here, token_step_inputs, kept, arrived),
        "tp",
        split_axis=0,
        concat_axis=0,
        tiled=True,
    )
    return attend(cache_length, queries, key_value_cache, adapter, bases)


def solution(mesh):
    in_specs = (
        P(None, ("group", "dp"), "tp"),
        P("tp", None),
        P(("group", "dp"), None, "tp"),
        P(("group", "dp"), None, "tp"),
        P(),
        P(None, ("group", "dp", "tp"), None),
        P(("group", "dp", "tp"), None, None),
        P(("group", "dp", "tp")),
    )
    out_specs = P(None, ("group", "dp", "tp"), None)
    return jax.shard_map(shards, mesh=mesh, in_specs=in_specs, out_specs=out_specs, check_vma=False)
```

```python
import math

import jax
import jax.numpy as jnp
from jax import lax
from jax.experimental import pallas as pl
from jax.experimental.pallas import tpu as pltpu
from jax.sharding import PartitionSpec as P

KVH = 8
HD = 128
GROUP = 16
STEPS = 8
OWN_ROWS = 8
TOKENS = STEPS * OWN_ROWS
CACHED = 32
MODEL_SHARD = 1024
RANK = 64
HALF_WIDTH = KVH * HD
PART_ORDERS = (("x", "u", "v"), ("v", "x", "u"))
MASKED = -1e30
SCORE_SCALE = math.log2(math.e) / math.sqrt(HD)
MIB = 1 << 20
LOW_ROWS = TOKENS // 2
MIDDLE = RANK // 2
SMALL_COST = pl.CostEstimate(flops=1, bytes_accessed=1, transcendentals=0)


def after(array, *earlier):
    return lax.optimization_barrier((array, *earlier))[0]


def tp_position(x, y, core):
    return (x * 4 + y) * 2 + core


def tp_pairs(move):
    return [
        (tp_position(x, y, core), tp_position(*move(x, y, core)))
        for x in range(2)
        for y in range(4)
        for core in range(2)
    ]


PAIRS = {
    "core": tp_pairs(lambda x, y, core: (x, y, 1 - core)),
    "x": tp_pairs(lambda x, y, core: (1 - x, y, core)),
    "u": tp_pairs(lambda x, y, core: (x, y ^ 1, core)),
    "v": tp_pairs(lambda x, y, core: (x, 3 - y, core)),
}
RING = (0, 1, 3, 2)


def swap(array, dim):
    return lax.ppermute(array, "tp", PAIRS[dim])


def project_kernel(core_ref, inputs_ref, weight_ref, keep_ref, send_ref):
    first = core_ref[0] == 0
    product = jnp.dot(
        inputs_ref[...].reshape(STEPS * 128, MODEL_SHARD),
        weight_ref[...],
        preferred_element_type=jnp.float32,
    )
    width = product.shape[1]
    product = product.reshape(STEPS, 8, 2, OWN_ROWS, width)
    for x in range(2):
        for v in range(2):
            for u in range(2):
                chip = x * 4 + RING[v * 2 + u]
                even = product[:, chip, 0].reshape(TOKENS, width)
                odd = product[:, chip, 1].reshape(TOKENS, width)
                keep_ref[x, v, u] = jnp.where(first, even, odd)
                send_ref[x, v, u] = jnp.where(first, odd, even).astype(jnp.bfloat16)


def project(core, token_step_inputs, key_value_weight):
    block = 512
    width = key_value_weight.shape[1]
    out_shape = (2, 2, 2, TOKENS, width)
    out_spec = pl.BlockSpec((2, 2, 2, TOKENS, block), lambda n, core_ref: (0, 0, 0, 0, n))
    return pl.pallas_call(
        project_kernel,
        grid_spec=pltpu.PrefetchScalarGridSpec(
            num_scalar_prefetch=1,
            grid=(width // block,),
            in_specs=[
                pl.BlockSpec((STEPS, 128, MODEL_SHARD), lambda n, core_ref: (0, 0, 0)),
                pl.BlockSpec((MODEL_SHARD, block), lambda n, core_ref: (0, n)),
            ],
            out_specs=[out_spec, out_spec],
        ),
        out_shape=[
            jax.ShapeDtypeStruct(out_shape, jnp.float32),
            jax.ShapeDtypeStruct(out_shape, jnp.bfloat16),
        ],
        compiler_params=pltpu.CompilerParams(vmem_limit_bytes=60 * MIB),
        cost_estimate=SMALL_COST,
        name="project",
    )(core, token_step_inputs, key_value_weight)


AXIS_OF = {"x": 0, "v": 1, "u": 2}


def outgoing_sum(terms, part, step, bits):
    total = None
    for term in terms:
        starts, sizes = [0] * 5, list(term.shape)
        starts[4], sizes[4] = (part * HALF_WIDTH if sizes[4] > HALF_WIDTH else 0), HALF_WIDTH
        for index, dim in enumerate(PART_ORDERS[part][: step + 1]):
            axis = AXIS_OF[dim]
            if sizes[axis] == 2:
                starts[axis] = bits[dim] if index < step else 1 - bits[dim]
                sizes[axis] = 1
        piece = lax.dynamic_slice(term, starts, sizes).astype(jnp.float32)
        total = piece if total is None else total + piece
    return total.astype(jnp.bfloat16)


def own_sum(terms, part, bits):
    total = None
    for term in terms:
        starts, sizes = [0] * 5, [1, 1, 1, TOKENS, HALF_WIDTH]
        starts[4] = part * HALF_WIDTH if term.shape[4] > HALF_WIDTH else 0
        for dim, axis in AXIS_OF.items():
            if term.shape[axis] == 2:
                starts[axis] = bits[dim]
        piece = lax.dynamic_slice(term, starts, sizes).astype(jnp.float32)
        total = piece if total is None else total + piece
    return total.reshape(TOKENS, HALF_WIDTH)


def slots_kernel(owners_ref, place_ref, down_ref, up_ref, other_ref, *out_refs):
    group, dp = place_ref[0], place_ref[1]
    for offset in range(8):
        tenant = owners_ref[lax.rem(group + offset, 8) * 2 + dp]
        held = lax.rem(tenant, 4)
        own = tenant // 4 == group * 2 + dp
        others = tenant // 4 == group * 2 + 1 - dp
        other = other_ref[held]
        other = jnp.where(others, other, jnp.zeros_like(other))
        down = jnp.where(own, down_ref[held], other[:, :MODEL_SHARD])
        up = jnp.where(own, up_ref[held], other[:, MODEL_SHARD:])
        for ref, rows in (
            ((out_refs[4], slice(0, MIDDLE)), (out_refs[8], slice(MIDDLE, RANK)))
            if offset == 4
            else ((out_refs[offset], slice(0, RANK)),)
        ):
            ref[:, :MODEL_SHARD] = down[rows]
            ref[:, MODEL_SHARD:] = up[rows]


def factor_slots(owners, place, down, up, other):
    vmem = pl.BlockSpec(memory_space=pltpu.VMEM)
    smem = pl.BlockSpec(memory_space=pltpu.SMEM)
    width = MODEL_SHARD + HD
    slots = [jax.ShapeDtypeStruct((RANK, width), jnp.bfloat16) for _ in range(9)]
    slots[4] = slots[8] = jax.ShapeDtypeStruct((MIDDLE, width), jnp.bfloat16)
    return pl.pallas_call(
        slots_kernel,
        in_specs=[smem, smem, vmem, vmem, vmem],
        out_specs=[vmem] * 9,
        out_shape=slots,
        compiler_params=pltpu.CompilerParams(vmem_limit_bytes=16 * MIB),
        cost_estimate=SMALL_COST,
        name="factor_slots",
    )(owners, place, down, up, other)


UP_RING = [(i, (i + 1) % 8) for i in range(8)]
DOWN_RING = [(i, (i - 1) % 8) for i in range(8)]


def pass_on(upward, downward):
    return lax.ppermute(upward, "group", UP_RING), lax.ppermute(downward, "group", DOWN_RING)


def low_kernel(inputs_ref, own_ref, below_ref, above_ref, out_ref):
    factors = own_ref[...] + (below_ref[...] + above_ref[...])
    product = lax.dot_general(
        inputs_ref[...].reshape(STEPS * 128, MODEL_SHARD),
        factors[:, :MODEL_SHARD],
        (((1,), (1,)), ((), ())),
        preferred_element_type=jnp.float32,
    )
    product = product.reshape(STEPS, 16, OWN_ROWS, RANK)
    for device in range(16):
        rows = product[:, device].reshape(2, LOW_ROWS, RANK)
        rows = jnp.concatenate([rows[0], rows[1]], axis=1)
        coarse = rows.astype(jnp.bfloat16)
        out_ref[device, :LOW_ROWS] = coarse
        out_ref[device, LOW_ROWS:TOKENS] = (rows - coarse.astype(jnp.float32)).astype(jnp.bfloat16)
        out_ref[device, TOKENS:] = factors[:, MODEL_SHARD:]


def low_rank(token_step_inputs, factors):
    vmem = pl.BlockSpec(memory_space=pltpu.VMEM)
    return pl.pallas_call(
        low_kernel,
        in_specs=[vmem] * 4,
        out_specs=vmem,
        out_shape=jax.ShapeDtypeStruct((16, TOKENS + RANK, HD), jnp.bfloat16),
        compiler_params=pltpu.CompilerParams(vmem_limit_bytes=24 * MIB),
        cost_estimate=SMALL_COST,
        name="low_rank",
    )(token_step_inputs, *factors)


def fresh_heads(adapter_ref, base_ref, fresh_ref):
    low = jnp.zeros((LOW_ROWS, HD), jnp.float32)
    for device in range(16):
        term = adapter_ref[device, :TOKENS].astype(jnp.float32)
        low = low + (term[:LOW_ROWS] + term[LOW_ROWS:])
    low = jnp.concatenate([low[:, :RANK], low[:, RANK:]], axis=0)
    coarse = low.astype(jnp.bfloat16)
    fine = (low - coarse.astype(jnp.float32)).astype(jnp.bfloat16)
    both = jnp.concatenate([coarse, fine], axis=1)
    for index in range(2 * KVH):
        up = adapter_ref[index, TOKENS:]
        up = jnp.concatenate([up, up], axis=0)
        total = jnp.dot(both, up, preferred_element_type=jnp.float32)
        total = total + base_ref[:, index * HD : (index + 1) * HD]
        fresh_ref[index] = total.astype(jnp.bfloat16).astype(jnp.float32)


def attend_kernel(
    lengths_ref,
    adapter_hbm,
    base_hbm,
    queries_hbm,
    cache_hbm,
    out_hbm,
    adapter_ref,
    base_ref,
    queries_ref,
    cache_ref,
    out_ref,
    fresh_ref,
    queries_wide_ref,
    out_wide_ref,
    whole_sem,
    queries_sem,
    out_sem,
):
    def head_columns(head):
        return pl.ds(pl.multiple_of(head * (GROUP * HD), GROUP * HD), GROUP * HD)

    def load(head):
        return pltpu.make_async_copy(
            queries_hbm.at[:, :, head_columns(head)], queries_ref.at[head], queries_sem.at[head]
        )

    def store(head):
        return pltpu.make_async_copy(
            out_ref.at[head], out_hbm.at[:, :, head_columns(head)], out_sem.at[head]
        )

    whole_loads = [
        pltpu.make_async_copy(source, target, whole_sem.at[i])
        for i, (source, target) in enumerate(
            [(adapter_hbm, adapter_ref), (base_hbm, base_ref), (cache_hbm, cache_ref)]
        )
    ]
    for copy in whole_loads:
        copy.start()
    for head in range(KVH):
        load(head).start()
    for copy in whole_loads[:2]:
        copy.wait()
    fresh_heads(adapter_ref, base_ref, fresh_ref)
    whole_loads[2].wait()

    positions = CACHED + 2 * STEPS
    position = lax.broadcasted_iota(jnp.int32, (positions, GROUP * STEPS), 0)
    step = lax.broadcasted_iota(jnp.int32, (positions, GROUP * STEPS), 1) % STEPS
    fresh_admitted = (position >= CACHED) & (position - CACHED <= step)
    padding = jnp.zeros((STEPS, HD), jnp.float32)

    def one_head(head, _):
        def positions_of(index, m):
            column = pl.ds(pl.multiple_of(index * HD, HD), HD)
            fresh = fresh_ref[index, pl.ds(m, STEPS, stride=OWN_ROWS), :]
            fresh = jnp.concatenate([fresh, padding], axis=0).astype(jnp.bfloat16)
            return jnp.concatenate([cache_ref[m, :, column], fresh], axis=0)

        load(head).wait()
        for g in range(GROUP):
            queries = queries_ref[head, :, :, g * HD : (g + 1) * HD].astype(jnp.float32)
            queries_wide_ref[g] = queries.reshape(TOKENS, HD)
        scores = []
        for m in range(OWN_ROWS):
            queries = jnp.concatenate(
                [
                    queries_wide_ref[g, pl.ds(m, STEPS, stride=OWN_ROWS), :]
                    for g in range(GROUP)
                ],
                axis=0,
            ).astype(jnp.bfloat16)
            scores.append(
                lax.dot_general(
                    positions_of(head, m),
                    queries,
                    (((1,), (1,)), ((), ())),
                    preferred_element_type=jnp.float32,
                )
            )
        probs = []
        for m in range(OWN_ROWS):
            admitted = fresh_admitted | (position < lengths_ref[m])
            shifted = jnp.where(admitted, scores[m] * SCORE_SCALE, MASKED)
            shifted = jnp.exp2(shifted - shifted.max(0, keepdims=True))
            shifted = shifted * (1.0 / shifted.sum(0, keepdims=True))
            probs.append(shifted.T.astype(jnp.bfloat16))
        mixed = [
            jnp.dot(probs[m], positions_of(KVH + head, m), preferred_element_type=jnp.float32)
            for m in range(OWN_ROWS)
        ]
        for m in range(OWN_ROWS):
            for g in range(GROUP):
                out_wide_ref[g, pl.ds(m, STEPS, stride=OWN_ROWS), :] = mixed[m][
                    g * STEPS : (g + 1) * STEPS
                ]
        for g in range(GROUP):
            mixed_rows = out_wide_ref[g].reshape(STEPS, OWN_ROWS, HD)
            out_ref[head, :, :, g * HD : (g + 1) * HD] = mixed_rows.astype(jnp.bfloat16)
        store(head).start()
        return 0

    lax.fori_loop(0, KVH, one_head, 0)
    for head in range(KVH):
        store(head).wait()


def attend(lengths, queries, cache, adapter, base):
    anywhere = pl.BlockSpec(memory_space=pl.ANY)
    heads = pltpu.VMEM((KVH, STEPS, OWN_ROWS, GROUP * HD), jnp.bfloat16)
    wide = pltpu.VMEM((GROUP, TOKENS, HD), jnp.float32)
    return pl.pallas_call(
        attend_kernel,
        in_specs=[pl.BlockSpec(memory_space=pltpu.SMEM)] + [anywhere] * 4,
        out_specs=anywhere,
        out_shape=jax.ShapeDtypeStruct(queries.shape, jnp.bfloat16),
        scratch_shapes=[
            pltpu.VMEM(adapter.shape, adapter.dtype),
            pltpu.VMEM(base.shape, base.dtype),
            heads,
            pltpu.VMEM(cache.shape, cache.dtype),
            heads,
            pltpu.VMEM((2 * KVH, TOKENS, HD), jnp.float32),
            wide,
            wide,
            pltpu.SemaphoreType.DMA((3,)),
            pltpu.SemaphoreType.DMA((KVH,)),
            pltpu.SemaphoreType.DMA((KVH,)),
        ],
        compiler_params=pltpu.CompilerParams(vmem_limit_bytes=24 * MIB),
        cost_estimate=SMALL_COST,
        name="attend",
    )(lengths, adapter, base, queries, cache)


def shards(
    token_step_inputs,
    key_value_weight,
    adapter_down_factors,
    adapter_up_factors,
    block_owner_tenant,
    queries,
    key_value_cache,
    cache_length,
):
    group, dp, tp = (lax.axis_index(name) for name in ("group", "dp", "tp"))
    core, y, x = tp % 2, (tp // 2) % 4, tp // 8
    bits = {
        "x": x,
        "u": ((y == 1) | (y == 2)).astype(jnp.int32),
        "v": (y >= 2).astype(jnp.int32),
    }

    own_factors = jnp.concatenate([adapter_down_factors, adapter_up_factors], axis=2)
    other_factors = lax.ppermute(own_factors, "dp", [(0, 1), (1, 0)])
    keep, outgoing = project(core.reshape(1), token_step_inputs, key_value_weight)
    other_factors = after(other_factors, keep)
    received = swap(after(outgoing, other_factors), "core")
    slots = factor_slots(
        block_owner_tenant,
        jnp.stack([group, dp]),
        adapter_down_factors,
        adapter_up_factors,
        other_factors,
    )
    received = after(received, slots[0])
    terms = [[keep, received], [keep, received]]

    def sums(step):
        return [outgoing_sum(terms[part], part, step, bits) for part in range(2)]

    def exchange(step, outgoing):
        for part in range(2):
            terms[part].append(swap(outgoing[part], PART_ORDERS[part][step]))

    below, above = pass_on(slots[4], slots[8])
    outgoing = sums(0)
    below, above = after(below, *outgoing), after(above, *outgoing)
    upward = jnp.concatenate([slots[3][:MIDDLE] + below, slots[3][MIDDLE:]], axis=0)
    downward = jnp.concatenate([slots[5][:MIDDLE], slots[5][MIDDLE:] + above], axis=0)
    below, above = pass_on(upward, downward)
    exchange(0, outgoing)
    upward, downward = slots[2] + below, slots[6] + above
    below, above = pass_on(upward, downward)
    for part in range(2):
        terms[part][2] = after(terms[part][2], upward, downward)
    exchange(1, sums(1))
    upward, downward = slots[1] + below, slots[7] + above
    below, above = pass_on(upward, downward)
    low = low_rank(token_step_inputs, (slots[0], below, above))
    adapter = lax.all_to_all(low, "tp", split_axis=0, concat_axis=0, tiled=True)
    for part in range(2):
        terms[part][3] = after(terms[part][3], low)
    exchange(2, sums(2))
    base = jnp.concatenate([own_sum(terms[part], part, bits) for part in range(2)], axis=1)
    return attend(cache_length, queries, key_value_cache, adapter, base)


def solution(mesh):
    in_specs = (
        P(None, ("group", "dp"), "tp"),
        P("tp", None),
        P(("group", "dp"), None, "tp"),
        P(("group", "dp"), None, "tp"),
        P(),
        P(None, ("group", "dp", "tp"), None),
        P(("group", "dp", "tp"), None, None),
        P(("group", "dp", "tp")),
    )
    out_specs = P(None, ("group", "dp", "tp"), None)
    return jax.shard_map(shards, mesh=mesh, in_specs=in_specs, out_specs=out_specs, check_vma=False)
```

```python
import math

import jax
import jax.numpy as jnp
from jax import lax
from jax.experimental import pallas as pl
from jax.experimental.pallas import tpu as pltpu
from jax.sharding import PartitionSpec as P

KVH = 8
HD = 128
GROUP = 16
STEPS = 8
OWN_ROWS = 8
TOKENS = STEPS * OWN_ROWS
CACHED = 32
MODEL_SHARD = 1024
RANK = 64
HALF_WIDTH = KVH * HD
PART_ORDERS = (("x", "u", "v"), ("v", "x", "u"))
MASKED = -1e30
SCORE_SCALE = math.log2(math.e) / math.sqrt(HD)
MIB = 1 << 20
LOW_ROWS = TOKENS // 2
MIDDLE = RANK // 2
SMALL_COST = pl.CostEstimate(flops=1, bytes_accessed=1, transcendentals=0)


def after(array, *earlier):
    return lax.optimization_barrier((array, *earlier))[0]


def tp_position(x, y, core):
    return (x * 4 + y) * 2 + core


def tp_pairs(move):
    return [
        (tp_position(x, y, core), tp_position(*move(x, y, core)))
        for x in range(2)
        for y in range(4)
        for core in range(2)
    ]


PAIRS = {
    "core": tp_pairs(lambda x, y, core: (x, y, 1 - core)),
    "x": tp_pairs(lambda x, y, core: (1 - x, y, core)),
    "u": tp_pairs(lambda x, y, core: (x, y ^ 1, core)),
    "v": tp_pairs(lambda x, y, core: (x, 3 - y, core)),
}
RING = (0, 1, 3, 2)


def swap(array, dim):
    return lax.ppermute(array, "tp", PAIRS[dim])


def project_kernel(core_ref, inputs_ref, weight_ref, keep_ref, send_ref):
    first = core_ref[0] == 0
    product = jnp.dot(
        inputs_ref[...].reshape(STEPS * 128, MODEL_SHARD),
        weight_ref[...],
        preferred_element_type=jnp.float32,
    )
    width = product.shape[1]
    product = product.reshape(STEPS, 8, 2, OWN_ROWS, width)
    for x in range(2):
        for v in range(2):
            for u in range(2):
                chip = x * 4 + RING[v * 2 + u]
                even = product[:, chip, 0].reshape(TOKENS, width)
                odd = product[:, chip, 1].reshape(TOKENS, width)
                keep_ref[x, v, u] = jnp.where(first, even, odd)
                send_ref[x, v, u] = jnp.where(first, odd, even).astype(jnp.bfloat16)


def project(core, token_step_inputs, key_value_weight):
    block = 512
    width = key_value_weight.shape[1]
    out_shape = (2, 2, 2, TOKENS, width)
    out_spec = pl.BlockSpec((2, 2, 2, TOKENS, block), lambda n, core_ref: (0, 0, 0, 0, n))
    return pl.pallas_call(
        project_kernel,
        grid_spec=pltpu.PrefetchScalarGridSpec(
            num_scalar_prefetch=1,
            grid=(width // block,),
            in_specs=[
                pl.BlockSpec((STEPS, 128, MODEL_SHARD), lambda n, core_ref: (0, 0, 0)),
                pl.BlockSpec((MODEL_SHARD, block), lambda n, core_ref: (0, n)),
            ],
            out_specs=[out_spec, out_spec],
        ),
        out_shape=[
            jax.ShapeDtypeStruct(out_shape, jnp.float32),
            jax.ShapeDtypeStruct(out_shape, jnp.bfloat16),
        ],
        compiler_params=pltpu.CompilerParams(vmem_limit_bytes=60 * MIB),
        cost_estimate=SMALL_COST,
        name="project",
    )(core, token_step_inputs, key_value_weight)


AXIS_OF = {"x": 0, "v": 1, "u": 2}


def outgoing_sum(terms, part, step, bits):
    total = None
    for term in terms:
        starts, sizes = [0] * 5, list(term.shape)
        starts[4], sizes[4] = (part * HALF_WIDTH if sizes[4] > HALF_WIDTH else 0), HALF_WIDTH
        for index, dim in enumerate(PART_ORDERS[part][: step + 1]):
            axis = AXIS_OF[dim]
            if sizes[axis] == 2:
                starts[axis] = bits[dim] if index < step else 1 - bits[dim]
                sizes[axis] = 1
        piece = lax.dynamic_slice(term, starts, sizes).astype(jnp.float32)
        total = piece if total is None else total + piece
    return total.astype(jnp.bfloat16)


def own_sum(terms, part, bits):
    total = None
    for term in terms:
        starts, sizes = [0] * 5, [1, 1, 1, TOKENS, HALF_WIDTH]
        starts[4] = part * HALF_WIDTH if term.shape[4] > HALF_WIDTH else 0
        for dim, axis in AXIS_OF.items():
            if term.shape[axis] == 2:
                starts[axis] = bits[dim]
        piece = lax.dynamic_slice(term, starts, sizes).astype(jnp.float32)
        total = piece if total is None else total + piece
    return total.reshape(TOKENS, HALF_WIDTH)


def slots_kernel(owners_ref, place_ref, down_ref, up_ref, other_ref, *out_refs):
    group, dp = place_ref[0], place_ref[1]
    for offset in range(8):
        tenant = owners_ref[lax.rem(group + offset, 8) * 2 + dp]
        held = lax.rem(tenant, 4)
        own = tenant // 4 == group * 2 + dp
        others = tenant // 4 == group * 2 + 1 - dp
        other = other_ref[held]
        other = jnp.where(others, other, jnp.zeros_like(other))
        down = jnp.where(own, down_ref[held], other[:, :MODEL_SHARD])
        up = jnp.where(own, up_ref[held], other[:, MODEL_SHARD:])
        for ref, rows in (
            ((out_refs[4], slice(0, MIDDLE)), (out_refs[8], slice(MIDDLE, RANK)))
            if offset == 4
            else ((out_refs[offset], slice(0, RANK)),)
        ):
            ref[:, :MODEL_SHARD] = down[rows]
            ref[:, MODEL_SHARD:] = up[rows]


def factor_slots(owners, place, down, up, other):
    vmem = pl.BlockSpec(memory_space=pltpu.VMEM)
    smem = pl.BlockSpec(memory_space=pltpu.SMEM)
    width = MODEL_SHARD + HD
    slots = [jax.ShapeDtypeStruct((RANK, width), jnp.bfloat16) for _ in range(9)]
    slots[4] = slots[8] = jax.ShapeDtypeStruct((MIDDLE, width), jnp.bfloat16)
    return pl.pallas_call(
        slots_kernel,
        in_specs=[smem, smem, vmem, vmem, vmem],
        out_specs=[vmem] * 9,
        out_shape=slots,
        compiler_params=pltpu.CompilerParams(vmem_limit_bytes=16 * MIB),
        cost_estimate=SMALL_COST,
        name="factor_slots",
    )(owners, place, down, up, other)


UP_RING = [(i, (i + 1) % 8) for i in range(8)]
DOWN_RING = [(i, (i - 1) % 8) for i in range(8)]


def pass_on(upward, downward):
    return lax.ppermute(upward, "group", UP_RING), lax.ppermute(downward, "group", DOWN_RING)


def low_kernel(inputs_ref, own_ref, below_ref, above_ref, out_ref):
    factors = own_ref[...] + (below_ref[...] + above_ref[...])
    product = lax.dot_general(
        inputs_ref[...].reshape(STEPS * 128, MODEL_SHARD),
        factors[:, :MODEL_SHARD],
        (((1,), (1,)), ((), ())),
        preferred_element_type=jnp.float32,
    )
    product = product.reshape(STEPS, 16, OWN_ROWS, RANK)
    for device in range(16):
        rows = product[:, device].reshape(2, LOW_ROWS, RANK)
        rows = jnp.concatenate([rows[0], rows[1]], axis=1)
        coarse = rows.astype(jnp.bfloat16)
        out_ref[device, :LOW_ROWS] = coarse
        out_ref[device, LOW_ROWS:TOKENS] = (rows - coarse.astype(jnp.float32)).astype(jnp.bfloat16)
        out_ref[device, TOKENS:] = factors[:, MODEL_SHARD:]


def low_rank(token_step_inputs, factors):
    vmem = pl.BlockSpec(memory_space=pltpu.VMEM)
    return pl.pallas_call(
        low_kernel,
        in_specs=[vmem] * 4,
        out_specs=vmem,
        out_shape=jax.ShapeDtypeStruct((16, TOKENS + RANK, HD), jnp.bfloat16),
        compiler_params=pltpu.CompilerParams(vmem_limit_bytes=24 * MIB),
        cost_estimate=SMALL_COST,
        name="low_rank",
    )(token_step_inputs, *factors)


def fresh_heads(adapter_ref, base_ref, fresh_ref):
    low = jnp.zeros((LOW_ROWS, HD), jnp.float32)
    for device in range(16):
        term = adapter_ref[device, :TOKENS].astype(jnp.float32)
        low = low + (term[:LOW_ROWS] + term[LOW_ROWS:])
    low = jnp.concatenate([low[:, :RANK], low[:, RANK:]], axis=0)
    coarse = low.astype(jnp.bfloat16)
    fine = (low - coarse.astype(jnp.float32)).astype(jnp.bfloat16)
    both = jnp.concatenate([coarse, fine], axis=1)
    for index in range(2 * KVH):
        up = adapter_ref[index, TOKENS:]
        up = jnp.concatenate([up, up], axis=0)
        total = jnp.dot(both, up, preferred_element_type=jnp.float32)
        total = total + base_ref[:, index * HD : (index + 1) * HD]
        fresh_ref[index] = total.astype(jnp.bfloat16).astype(jnp.float32)


def attend_kernel(
    lengths_ref,
    adapter_hbm,
    base_hbm,
    queries_hbm,
    cache_hbm,
    out_hbm,
    adapter_ref,
    base_ref,
    queries_ref,
    cache_ref,
    out_ref,
    fresh_ref,
    queries_wide_ref,
    out_wide_ref,
    whole_sem,
    queries_sem,
    out_sem,
):
    def head_columns(head):
        return pl.ds(pl.multiple_of(head * (GROUP * HD), GROUP * HD), GROUP * HD)

    def load(head):
        return pltpu.make_async_copy(
            queries_hbm.at[:, :, head_columns(head)], queries_ref.at[head], queries_sem.at[head]
        )

    def store(head):
        return pltpu.make_async_copy(
            out_ref.at[head], out_hbm.at[:, :, head_columns(head)], out_sem.at[head]
        )

    whole_loads = [
        pltpu.make_async_copy(source, target, whole_sem.at[i])
        for i, (source, target) in enumerate(
            [(adapter_hbm, adapter_ref), (base_hbm, base_ref), (cache_hbm, cache_ref)]
        )
    ]
    for copy in whole_loads:
        copy.start()
    for head in range(KVH):
        load(head).start()
    for copy in whole_loads[:2]:
        copy.wait()
    fresh_heads(adapter_ref, base_ref, fresh_ref)
    whole_loads[2].wait()

    positions = CACHED + 2 * STEPS
    position = lax.broadcasted_iota(jnp.int32, (positions, GROUP * STEPS), 0)
    step = lax.broadcasted_iota(jnp.int32, (positions, GROUP * STEPS), 1) % STEPS
    fresh_admitted = (position >= CACHED) & (position - CACHED <= step)
    padding = jnp.zeros((STEPS, HD), jnp.float32)

    def one_head(head, _):
        def positions_of(index, m):
            column = pl.ds(pl.multiple_of(index * HD, HD), HD)
            fresh = fresh_ref[index, pl.ds(m, STEPS, stride=OWN_ROWS), :]
            fresh = jnp.concatenate([fresh, padding], axis=0).astype(jnp.bfloat16)
            return jnp.concatenate([cache_ref[m, :, column], fresh], axis=0)

        load(head).wait()
        for g in range(GROUP):
            queries = queries_ref[head, :, :, g * HD : (g + 1) * HD].astype(jnp.float32)
            queries_wide_ref[g] = queries.reshape(TOKENS, HD)
        scores = []
        for m in range(OWN_ROWS):
            queries = jnp.concatenate(
                [
                    queries_wide_ref[g, pl.ds(m, STEPS, stride=OWN_ROWS), :]
                    for g in range(GROUP)
                ],
                axis=0,
            ).astype(jnp.bfloat16)
            scores.append(
                lax.dot_general(
                    positions_of(head, m),
                    queries,
                    (((1,), (1,)), ((), ())),
                    preferred_element_type=jnp.float32,
                )
            )
        probs = []
        for m in range(OWN_ROWS):
            admitted = fresh_admitted | (position < lengths_ref[m])
            shifted = jnp.where(admitted, scores[m] * SCORE_SCALE, MASKED)
            shifted = jnp.exp2(shifted - shifted.max(0, keepdims=True))
            shifted = shifted * (1.0 / shifted.sum(0, keepdims=True))
            probs.append(shifted.T.astype(jnp.bfloat16))
        mixed = [
            jnp.dot(probs[m], positions_of(KVH + head, m), preferred_element_type=jnp.float32)
            for m in range(OWN_ROWS)
        ]
        for m in range(OWN_ROWS):
            for g in range(GROUP):
                out_wide_ref[g, pl.ds(m, STEPS, stride=OWN_ROWS), :] = mixed[m][
                    g * STEPS : (g + 1) * STEPS
                ]
        for g in range(GROUP):
            mixed_rows = out_wide_ref[g].reshape(STEPS, OWN_ROWS, HD)
            out_ref[head, :, :, g * HD : (g + 1) * HD] = mixed_rows.astype(jnp.bfloat16)
        store(head).start()
        return 0

    lax.fori_loop(0, KVH, one_head, 0)
    for head in range(KVH):
        store(head).wait()


def attend(lengths, queries, cache, adapter, base):
    anywhere = pl.BlockSpec(memory_space=pl.ANY)
    heads = pltpu.VMEM((KVH, STEPS, OWN_ROWS, GROUP * HD), jnp.bfloat16)
    wide = pltpu.VMEM((GROUP, TOKENS, HD), jnp.float32)
    return pl.pallas_call(
        attend_kernel,
        in_specs=[pl.BlockSpec(memory_space=pltpu.SMEM)] + [anywhere] * 4,
        out_specs=anywhere,
        out_shape=jax.ShapeDtypeStruct(queries.shape, jnp.bfloat16),
        scratch_shapes=[
            pltpu.VMEM(adapter.shape, adapter.dtype),
            pltpu.VMEM(base.shape, base.dtype),
            heads,
            pltpu.VMEM(cache.shape, cache.dtype),
            heads,
            pltpu.VMEM((2 * KVH, TOKENS, HD), jnp.float32),
            wide,
            wide,
            pltpu.SemaphoreType.DMA((3,)),
            pltpu.SemaphoreType.DMA((KVH,)),
            pltpu.SemaphoreType.DMA((KVH,)),
        ],
        compiler_params=pltpu.CompilerParams(vmem_limit_bytes=24 * MIB),
        cost_estimate=SMALL_COST,
        name="attend",
    )(lengths, adapter, base, queries, cache)


def shards(
    token_step_inputs,
    key_value_weight,
    adapter_down_factors,
    adapter_up_factors,
    block_owner_tenant,
    queries,
    key_value_cache,
    cache_length,
):
    group, dp, tp = (lax.axis_index(name) for name in ("group", "dp", "tp"))
    core, y, x = tp % 2, (tp // 2) % 4, tp // 8
    bits = {
        "x": x,
        "u": ((y == 1) | (y == 2)).astype(jnp.int32),
        "v": (y >= 2).astype(jnp.int32),
    }

    own_factors = jnp.concatenate([adapter_down_factors, adapter_up_factors], axis=2)
    other_factors = lax.ppermute(own_factors, "dp", [(0, 1), (1, 0)])
    keep, outgoing = project(core.reshape(1), token_step_inputs, key_value_weight)
    other_factors = after(other_factors, keep)
    received = swap(after(outgoing, other_factors), "core")
    slots = factor_slots(
        block_owner_tenant,
        jnp.stack([group, dp]),
        adapter_down_factors,
        adapter_up_factors,
        other_factors,
    )
    received = after(received, slots[0])
    terms = [[keep, received], [keep, received]]

    def next_sum(part, *earlier):
        terms[part][-1] = after(terms[part][-1], *earlier)
        return outgoing_sum(terms[part], part, len(terms[part]) - 2, bits)

    def exchange(part, outgoing):
        terms[part].append(swap(outgoing, PART_ORDERS[part][len(terms[part]) - 2]))
        return outgoing

    below, above = pass_on(slots[4], slots[8])
    outgoing = [next_sum(part) for part in range(2)]
    below, above = after(below, *outgoing), after(above, *outgoing)
    upward = jnp.concatenate([slots[3][:MIDDLE] + below, slots[3][MIDDLE:]], axis=0)
    downward = jnp.concatenate([slots[5][:MIDDLE], slots[5][MIDDLE:] + above], axis=0)
    below, above = pass_on(upward, downward)
    for part in range(2):
        exchange(part, outgoing[part])
    upward, downward = slots[2] + below, slots[6] + above
    below, above = pass_on(upward, downward)
    sent = exchange(1, next_sum(1, upward, downward))
    sent = exchange(0, next_sum(0, sent))
    below, above = after(below, sent), after(above, sent)
    upward, downward = slots[1] + below, slots[7] + above
    below, above = pass_on(upward, downward)
    sent = exchange(1, next_sum(1, upward, downward))
    sent = exchange(0, next_sum(0, sent))
    low = low_rank(token_step_inputs, (slots[0], after(below, sent), above))
    adapter = lax.all_to_all(low, "tp", split_axis=0, concat_axis=0, tiled=True)
    base = jnp.concatenate([own_sum(terms[part], part, bits) for part in range(2)], axis=1)
    return attend(cache_length, queries, key_value_cache, adapter, base)


def solution(mesh):
    in_specs = (
        P(None, ("group", "dp"), "tp"),
        P("tp", None),
        P(("group", "dp"), None, "tp"),
        P(("group", "dp"), None, "tp"),
        P(),
        P(None, ("group", "dp", "tp"), None),
        P(("group", "dp", "tp"), None, None),
        P(("group", "dp", "tp")),
    )
    out_specs = P(None, ("group", "dp", "tp"), None)
    return jax.shard_map(shards, mesh=mesh, in_specs=in_specs, out_specs=out_specs, check_vma=False)
```

```python
import math

import jax
import jax.numpy as jnp
from jax import lax
from jax.experimental import pallas as pl
from jax.experimental.pallas import tpu as pltpu
from jax.sharding import PartitionSpec as P

KVH = 8
HD = 128
GROUP = 16
STEPS = 8
OWN_ROWS = 8
TOKENS = STEPS * OWN_ROWS
CACHED = 32
MODEL_SHARD = 1024
RANK = 64
HALF_WIDTH = KVH * HD
PART_ORDERS = (("x", "u", "v"), ("v", "x", "u"))
MASKED = -1e30
SCORE_SCALE = math.log2(math.e) / math.sqrt(HD)
MIB = 1 << 20
LOW_ROWS = TOKENS // 2
MIDDLE = RANK // 2
SMALL_COST = pl.CostEstimate(flops=1, bytes_accessed=1, transcendentals=0)


def after(array, *earlier):
    return lax.optimization_barrier((array, *earlier))[0]


def tp_position(x, y, core):
    return (x * 4 + y) * 2 + core


def tp_pairs(move):
    return [
        (tp_position(x, y, core), tp_position(*move(x, y, core)))
        for x in range(2)
        for y in range(4)
        for core in range(2)
    ]


PAIRS = {
    "core": tp_pairs(lambda x, y, core: (x, y, 1 - core)),
    "x": tp_pairs(lambda x, y, core: (1 - x, y, core)),
    "u": tp_pairs(lambda x, y, core: (x, y ^ 1, core)),
    "v": tp_pairs(lambda x, y, core: (x, 3 - y, core)),
}
RING = (0, 1, 3, 2)


def swap(array, dim):
    return lax.ppermute(array, "tp", PAIRS[dim])


def project_kernel(core_ref, inputs_ref, weight_ref, keep_ref, send_ref):
    first = core_ref[0] == 0
    product = jnp.dot(
        inputs_ref[...].reshape(STEPS * 128, MODEL_SHARD),
        weight_ref[...],
        preferred_element_type=jnp.float32,
    )
    width = product.shape[1]
    product = product.reshape(STEPS, 8, 2, OWN_ROWS, width)
    for x in range(2):
        for v in range(2):
            for u in range(2):
                chip = x * 4 + RING[v * 2 + u]
                even = product[:, chip, 0].reshape(TOKENS, width)
                odd = product[:, chip, 1].reshape(TOKENS, width)
                keep_ref[x, v, u] = jnp.where(first, even, odd)
                send_ref[x, v, u] = jnp.where(first, odd, even).astype(jnp.bfloat16)


def project(core, token_step_inputs, key_value_weight):
    block = 512
    width = key_value_weight.shape[1]
    out_shape = (2, 2, 2, TOKENS, width)
    out_spec = pl.BlockSpec((2, 2, 2, TOKENS, block), lambda n, core_ref: (0, 0, 0, 0, n))
    return pl.pallas_call(
        project_kernel,
        grid_spec=pltpu.PrefetchScalarGridSpec(
            num_scalar_prefetch=1,
            grid=(width // block,),
            in_specs=[
                pl.BlockSpec((STEPS, 128, MODEL_SHARD), lambda n, core_ref: (0, 0, 0)),
                pl.BlockSpec((MODEL_SHARD, block), lambda n, core_ref: (0, n)),
            ],
            out_specs=[out_spec, out_spec],
        ),
        out_shape=[
            jax.ShapeDtypeStruct(out_shape, jnp.float32),
            jax.ShapeDtypeStruct(out_shape, jnp.bfloat16),
        ],
        compiler_params=pltpu.CompilerParams(vmem_limit_bytes=60 * MIB),
        cost_estimate=SMALL_COST,
        name="project",
    )(core, token_step_inputs, key_value_weight)


AXIS_OF = {"x": 0, "v": 1, "u": 2}


def outgoing_sum(terms, part, step, bits):
    total = None
    for term in terms:
        starts, sizes = [0] * 5, list(term.shape)
        starts[4], sizes[4] = (part * HALF_WIDTH if sizes[4] > HALF_WIDTH else 0), HALF_WIDTH
        for index, dim in enumerate(PART_ORDERS[part][: step + 1]):
            axis = AXIS_OF[dim]
            if sizes[axis] == 2:
                starts[axis] = bits[dim] if index < step else 1 - bits[dim]
                sizes[axis] = 1
        piece = lax.dynamic_slice(term, starts, sizes).astype(jnp.float32)
        total = piece if total is None else total + piece
    return total.astype(jnp.bfloat16)


def own_sum(terms, part, bits):
    total = None
    for term in terms:
        starts, sizes = [0] * 5, [1, 1, 1, TOKENS, HALF_WIDTH]
        starts[4] = part * HALF_WIDTH if term.shape[4] > HALF_WIDTH else 0
        for dim, axis in AXIS_OF.items():
            if term.shape[axis] == 2:
                starts[axis] = bits[dim]
        piece = lax.dynamic_slice(term, starts, sizes).astype(jnp.float32)
        total = piece if total is None else total + piece
    return total.reshape(TOKENS, HALF_WIDTH)


def slots_kernel(owners_ref, place_ref, down_ref, up_ref, other_ref, *out_refs):
    group, dp = place_ref[0], place_ref[1]
    for offset in range(8):
        tenant = owners_ref[lax.rem(group + offset, 8) * 2 + dp]
        held = lax.rem(tenant, 4)
        own = tenant // 4 == group * 2 + dp
        others = tenant // 4 == group * 2 + 1 - dp
        other = other_ref[held]
        other = jnp.where(others, other, jnp.zeros_like(other))
        down = jnp.where(own, down_ref[held], other[:, :MODEL_SHARD])
        up = jnp.where(own, up_ref[held], other[:, MODEL_SHARD:])
        for ref, rows in (
            ((out_refs[4], slice(0, MIDDLE)), (out_refs[8], slice(MIDDLE, RANK)))
            if offset == 4
            else ((out_refs[offset], slice(0, RANK)),)
        ):
            ref[:, :MODEL_SHARD] = down[rows]
            ref[:, MODEL_SHARD:] = up[rows]


def factor_slots(owners, place, down, up, other):
    vmem = pl.BlockSpec(memory_space=pltpu.VMEM)
    smem = pl.BlockSpec(memory_space=pltpu.SMEM)
    width = MODEL_SHARD + HD
    slots = [jax.ShapeDtypeStruct((RANK, width), jnp.bfloat16) for _ in range(9)]
    slots[4] = slots[8] = jax.ShapeDtypeStruct((MIDDLE, width), jnp.bfloat16)
    return pl.pallas_call(
        slots_kernel,
        in_specs=[smem, smem, vmem, vmem, vmem],
        out_specs=[vmem] * 9,
        out_shape=slots,
        compiler_params=pltpu.CompilerParams(vmem_limit_bytes=16 * MIB),
        cost_estimate=SMALL_COST,
        name="factor_slots",
    )(owners, place, down, up, other)


UP_RING = [(i, (i + 1) % 8) for i in range(8)]
DOWN_RING = [(i, (i - 1) % 8) for i in range(8)]


def pass_on(upward, downward):
    return lax.ppermute(upward, "group", UP_RING), lax.ppermute(downward, "group", DOWN_RING)


def low_kernel(inputs_ref, own_ref, below_ref, above_ref, out_ref):
    factors = own_ref[...] + (below_ref[...] + above_ref[...])
    product = lax.dot_general(
        inputs_ref[...].reshape(STEPS * 128, MODEL_SHARD),
        factors[:, :MODEL_SHARD],
        (((1,), (1,)), ((), ())),
        preferred_element_type=jnp.float32,
    )
    product = product.reshape(STEPS, 16, OWN_ROWS, RANK)
    for device in range(16):
        rows = product[:, device].reshape(2, LOW_ROWS, RANK)
        rows = jnp.concatenate([rows[0], rows[1]], axis=1)
        coarse = rows.astype(jnp.bfloat16)
        out_ref[device, :LOW_ROWS] = coarse
        out_ref[device, LOW_ROWS:TOKENS] = (rows - coarse.astype(jnp.float32)).astype(jnp.bfloat16)
        out_ref[device, TOKENS:] = factors[:, MODEL_SHARD:]


def low_rank(token_step_inputs, factors):
    vmem = pl.BlockSpec(memory_space=pltpu.VMEM)
    return pl.pallas_call(
        low_kernel,
        in_specs=[vmem] * 4,
        out_specs=vmem,
        out_shape=jax.ShapeDtypeStruct((16, TOKENS + RANK, HD), jnp.bfloat16),
        compiler_params=pltpu.CompilerParams(vmem_limit_bytes=24 * MIB),
        cost_estimate=SMALL_COST,
        name="low_rank",
    )(token_step_inputs, *factors)


def fresh_heads(adapter_ref, base_ref, fresh_ref):
    low = jnp.zeros((LOW_ROWS, HD), jnp.float32)
    for device in range(16):
        term = adapter_ref[device, :TOKENS].astype(jnp.float32)
        low = low + (term[:LOW_ROWS] + term[LOW_ROWS:])
    low = jnp.concatenate([low[:, :RANK], low[:, RANK:]], axis=0)
    coarse = low.astype(jnp.bfloat16)
    fine = (low - coarse.astype(jnp.float32)).astype(jnp.bfloat16)
    both = jnp.concatenate([coarse, fine], axis=1)
    for index in range(2 * KVH):
        up = adapter_ref[index, TOKENS:]
        up = jnp.concatenate([up, up], axis=0)
        total = jnp.dot(both, up, preferred_element_type=jnp.float32)
        total = total + base_ref[:, index * HD : (index + 1) * HD]
        fresh_ref[index] = total.astype(jnp.bfloat16).astype(jnp.float32)


def attend_kernel(
    lengths_ref,
    adapter_hbm,
    base_hbm,
    queries_hbm,
    cache_hbm,
    out_hbm,
    adapter_ref,
    base_ref,
    queries_ref,
    cache_ref,
    out_ref,
    fresh_ref,
    queries_wide_ref,
    out_wide_ref,
    whole_sem,
    queries_sem,
    out_sem,
):
    def head_columns(head):
        return pl.ds(pl.multiple_of(head * (GROUP * HD), GROUP * HD), GROUP * HD)

    def load(head):
        return pltpu.make_async_copy(
            queries_hbm.at[:, :, head_columns(head)], queries_ref.at[head], queries_sem.at[head]
        )

    def store(head):
        return pltpu.make_async_copy(
            out_ref.at[head], out_hbm.at[:, :, head_columns(head)], out_sem.at[head]
        )

    whole_loads = [
        pltpu.make_async_copy(source, target, whole_sem.at[i])
        for i, (source, target) in enumerate(
            [(adapter_hbm, adapter_ref), (base_hbm, base_ref), (cache_hbm, cache_ref)]
        )
    ]
    for copy in whole_loads:
        copy.start()
    for head in range(KVH):
        load(head).start()
    for copy in whole_loads[:2]:
        copy.wait()
    fresh_heads(adapter_ref, base_ref, fresh_ref)
    whole_loads[2].wait()

    positions = CACHED + 2 * STEPS
    position = lax.broadcasted_iota(jnp.int32, (positions, GROUP * STEPS), 0)
    step = lax.broadcasted_iota(jnp.int32, (positions, GROUP * STEPS), 1) % STEPS
    fresh_admitted = (position >= CACHED) & (position - CACHED <= step)
    padding = jnp.zeros((STEPS, HD), jnp.float32)

    def one_head(head, _):
        def positions_of(index, m):
            column = pl.ds(pl.multiple_of(index * HD, HD), HD)
            fresh = fresh_ref[index, pl.ds(m, STEPS, stride=OWN_ROWS), :]
            fresh = jnp.concatenate([fresh, padding], axis=0).astype(jnp.bfloat16)
            return jnp.concatenate([cache_ref[m, :, column], fresh], axis=0)

        load(head).wait()
        for g in range(GROUP):
            queries = queries_ref[head, :, :, g * HD : (g + 1) * HD].astype(jnp.float32)
            queries_wide_ref[g] = queries.reshape(TOKENS, HD)
        scores = []
        for m in range(OWN_ROWS):
            queries = jnp.concatenate(
                [
                    queries_wide_ref[g, pl.ds(m, STEPS, stride=OWN_ROWS), :]
                    for g in range(GROUP)
                ],
                axis=0,
            ).astype(jnp.bfloat16)
            scores.append(
                lax.dot_general(
                    positions_of(head, m),
                    queries,
                    (((1,), (1,)), ((), ())),
                    preferred_element_type=jnp.float32,
                )
            )
        probs = []
        for m in range(OWN_ROWS):
            admitted = fresh_admitted | (position < lengths_ref[m])
            shifted = jnp.where(admitted, scores[m] * SCORE_SCALE, MASKED)
            shifted = jnp.exp2(shifted - shifted.max(0, keepdims=True))
            shifted = shifted * (1.0 / shifted.sum(0, keepdims=True))
            probs.append(shifted.T.astype(jnp.bfloat16))
        mixed = [
            jnp.dot(probs[m], positions_of(KVH + head, m), preferred_element_type=jnp.float32)
            for m in range(OWN_ROWS)
        ]
        for m in range(OWN_ROWS):
            for g in range(GROUP):
                out_wide_ref[g, pl.ds(m, STEPS, stride=OWN_ROWS), :] = mixed[m][
                    g * STEPS : (g + 1) * STEPS
                ]
        for g in range(GROUP):
            mixed_rows = out_wide_ref[g].reshape(STEPS, OWN_ROWS, HD)
            out_ref[head, :, :, g * HD : (g + 1) * HD] = mixed_rows.astype(jnp.bfloat16)
        store(head).start()
        return 0

    lax.fori_loop(0, KVH, one_head, 0)
    for head in range(KVH):
        store(head).wait()


def attend(lengths, queries, cache, adapter, base):
    anywhere = pl.BlockSpec(memory_space=pl.ANY)
    hbm = pl.BlockSpec(memory_space=pltpu.HBM)
    heads = pltpu.VMEM((KVH, STEPS, OWN_ROWS, GROUP * HD), jnp.bfloat16)
    wide = pltpu.VMEM((GROUP, TOKENS, HD), jnp.float32)
    return pl.pallas_call(
        attend_kernel,
        in_specs=[pl.BlockSpec(memory_space=pltpu.SMEM)] + [anywhere] * 2 + [hbm] * 2,
        out_specs=anywhere,
        out_shape=jax.ShapeDtypeStruct(queries.shape, jnp.bfloat16),
        scratch_shapes=[
            pltpu.VMEM(adapter.shape, adapter.dtype),
            pltpu.VMEM(base.shape, base.dtype),
            heads,
            pltpu.VMEM(cache.shape, cache.dtype),
            heads,
            pltpu.VMEM((2 * KVH, TOKENS, HD), jnp.float32),
            wide,
            wide,
            pltpu.SemaphoreType.DMA((3,)),
            pltpu.SemaphoreType.DMA((KVH,)),
            pltpu.SemaphoreType.DMA((KVH,)),
        ],
        compiler_params=pltpu.CompilerParams(vmem_limit_bytes=24 * MIB),
        cost_estimate=SMALL_COST,
        name="attend",
    )(lengths, adapter, base, queries, cache)


def shards(
    token_step_inputs,
    key_value_weight,
    adapter_down_factors,
    adapter_up_factors,
    block_owner_tenant,
    queries,
    key_value_cache,
    cache_length,
):
    group, dp, tp = (lax.axis_index(name) for name in ("group", "dp", "tp"))
    core, y, x = tp % 2, (tp // 2) % 4, tp // 8
    bits = {
        "x": x,
        "u": ((y == 1) | (y == 2)).astype(jnp.int32),
        "v": (y >= 2).astype(jnp.int32),
    }

    own_factors = jnp.concatenate([adapter_down_factors, adapter_up_factors], axis=2)
    other_factors = lax.ppermute(own_factors, "dp", [(0, 1), (1, 0)])
    keep, outgoing = project(core.reshape(1), token_step_inputs, key_value_weight)
    other_factors = after(other_factors, keep)
    received = swap(after(outgoing, other_factors), "core")
    slots = factor_slots(
        block_owner_tenant,
        jnp.stack([group, dp]),
        adapter_down_factors,
        adapter_up_factors,
        other_factors,
    )
    received = after(received, slots[0])
    terms = [[keep, received], [keep, received]]

    def next_sum(part, *earlier):
        terms[part][-1] = after(terms[part][-1], *earlier)
        return outgoing_sum(terms[part], part, len(terms[part]) - 2, bits)

    def exchange(part, outgoing):
        terms[part].append(swap(outgoing, PART_ORDERS[part][len(terms[part]) - 2]))
        return outgoing

    far_below = lax.ppermute(slots[4], "group", [(i, (i + 2) % 8) for i in range(8)])
    far_above = lax.ppermute(slots[8], "group", [(i, (i - 2) % 8) for i in range(8)])
    below, above = pass_on(slots[3], slots[5])
    outgoing = [next_sum(part) for part in range(2)]
    below, above = after(below, *outgoing), after(above, *outgoing)
    upward, downward = slots[2] + below, slots[6] + above
    upward = jnp.concatenate([upward[:MIDDLE] + far_below, upward[MIDDLE:]], axis=0)
    downward = jnp.concatenate([downward[:MIDDLE], downward[MIDDLE:] + far_above], axis=0)
    below, above = pass_on(upward, downward)
    for part in range(2):
        exchange(part, outgoing[part])
    upward, downward = slots[1] + below, slots[7] + above
    below, above = pass_on(upward, downward)
    sent = exchange(1, next_sum(1, upward, downward))
    sent = exchange(0, next_sum(0, sent))
    sent = exchange(1, next_sum(1, sent))
    sent = exchange(0, next_sum(0, sent))
    low = low_rank(token_step_inputs, (slots[0], after(below, sent), above))
    adapter = lax.all_to_all(low, "tp", split_axis=0, concat_axis=0, tiled=True)
    base = jnp.concatenate([own_sum(terms[part], part, bits) for part in range(2)], axis=1)
    return attend(cache_length, queries, key_value_cache, adapter, base)


def solution(mesh):
    in_specs = (
        P(None, ("group", "dp"), "tp"),
        P("tp", None),
        P(("group", "dp"), None, "tp"),
        P(("group", "dp"), None, "tp"),
        P(),
        P(None, ("group", "dp", "tp"), None),
        P(("group", "dp", "tp"), None, None),
        P(("group", "dp", "tp")),
    )
    out_specs = P(None, ("group", "dp", "tp"), None)
    return jax.shard_map(shards, mesh=mesh, in_specs=in_specs, out_specs=out_specs, check_vma=False)
```
